512 devices in a mesh: grp: 16 (over z), pair: 32 (over x, y, core).
Axes of the slice: x: 4, y: 4, z: 16, core: 2. Of those that a mesh axis runs over, the one named last changes fastest.
Arguments:
- orbital_ints: bfloat16 [1024, 256, 256], P(('grp', 'pair')), may hold values from -1.5 to 1.5
- pair_fock: float32 [16384, 2], P(('grp', 'pair')), may hold values from -2 to -0.2
- pair_orbitals: int32 [16384, 2], P(('grp', 'pair')), may hold values from 0 to 1023, as said below
- rank_bucket: int32 [16384], P(('grp', 'pair')), may hold values from 1 to 3
- pno_coeffs: bfloat16 [16384, 256, 96], P(('grp', 'pair')), may hold values from -0.375 to 0.375
- pno_energy: float32 [16384, 96], P(('grp', 'pair')), may hold values from 0.2 to 4
- amplitudes: bfloat16 [16384, 96, 96], P(('grp', 'pair')), may hold values from -1.796875 to 1.796875
- neighbors: int32 [16384, 2], P(('grp', 'pair')), may hold values from 0 to 16383, as said below
- intersections: bfloat16 [16384, 2, 96, 96], P(('grp', 'pair')), may hold values from -1.1953125 to 1.1953125
- coupling_fock: float32 [16384, 2], P(('grp', 'pair')), may hold values from -4 to 4
Outputs:
- residual: float32 [16384, 96, 96], P(('grp', 'pair'))
The draws below stay inside these ranges and needn't reach their ends.
Inputs may be any that keep to these rules, and one draw needn't show every extreme that they name: `pair_orbitals`: pair p's first orbital is held by the device that owns pair p. Its second orbital is held by the device with the same pair index in some grp group. Among the pairs of one device, at most 4 have their second orbital in any one group, and exactly 4 in some group. `neighbors`: neighbor pairs belong to the same grp group as the pair. Among the 64 references of the rows of one device, at most 4 point to pairs of any one device, and exactly 4 to some device.
All inputs are finite; a program needn't handle non-finite values.
Results may differ from the reference program's by a relative error of at most 0.0055.
Values may be sent and summed in bfloat16 or wider, within the bound.
A program may use at most 128 MiB of HBM per device.

```python
import math
import jax
import jax.numpy as jnp
from jax import lax

NV = 256
NAUX = 256
R = 96
NB = 2
PAIR_DEV = 32
ORB_DEV = 2
PAIRS = 16384
ORBS = 1024
N_GRP = 16
N_PAIR = 32
DEVICES = 512


def capped_targets(slot_key, fill_key, shuffle_key, peer_count, capacity, wanted_count):
    full_peer = jax.random.randint(fill_key, (), 0, peer_count)
    slot_list = jax.random.permutation(slot_key, peer_count * capacity)
    slot_order = jnp.argsort((slot_list // capacity != full_peer).astype(jnp.int32), stable=True)
    chosen = slot_list[slot_order][:wanted_count]
    chosen = jax.random.permutation(shuffle_key, chosen)
    return (chosen // capacity).astype(jnp.int32)


def draw_pair_orbitals(key, part):
    key = jax.random.fold_in(key, 11)
    capacity = max(2, 2 * PAIR_DEV // N_GRP)

    def one_device(device):
        device_key = jax.random.fold_in(key, device)
        key_first, key_slots, key_fill, key_shuffle, key_second = jax.random.split(device_key, 5)
        column = device % N_PAIR
        first_orbital = device * ORB_DEV + jax.random.randint(key_first, (PAIR_DEV,), 0, ORB_DEV)
        owner_group = capped_targets(key_slots, key_fill, key_shuffle, N_GRP, capacity, PAIR_DEV)
        second_orbital = (owner_group * N_PAIR + column) * ORB_DEV + jax.random.randint(key_second, (PAIR_DEV,), 0, ORB_DEV)
        return jnp.stack([first_orbital, second_orbital], axis=1)
    result = jax.vmap(one_device)(jnp.arange(DEVICES, dtype=jnp.int32))
    return result.reshape(DEVICES * PAIR_DEV, 2).astype(jnp.int32)


def draw_neighbors(key, part):
    key = jax.random.fold_in(key, 23)
    capacity = max(2, 2 * PAIR_DEV * NB // N_PAIR)

    def one_device(device):
        device_key = jax.random.fold_in(key, device)
        key_slots, key_fill, key_shuffle, key_local = jax.random.split(device_key, 4)
        group_index = device // N_PAIR
        target_column = capped_targets(key_slots, key_fill, key_shuffle, N_PAIR, capacity, PAIR_DEV * NB)
        target_local = jax.random.randint(key_local, (PAIR_DEV * NB,), 0, PAIR_DEV)
        return (group_index * N_PAIR + target_column) * PAIR_DEV + target_local
    result = jax.vmap(one_device)(jnp.arange(DEVICES, dtype=jnp.int32))
    return result.reshape(DEVICES * PAIR_DEV, NB).astype(jnp.int32)


def with_ends(drawn, stream_key, low, largest):
    extent = drawn.shape
    spot = [jax.random.randint(jax.random.fold_in(stream_key, axis), (), 0, extent[axis]) for axis in range(len(extent))]
    drawn = drawn.at[tuple(spot)].set(low)
    longest = extent.index(max(extent))
    spot[longest] = (spot[longest] + 1) % extent[longest]
    return drawn.at[tuple(spot)].set(largest)


def block_levels(own_key, shape, shards, low, high):
    loudness, own = 1.0, jax.random.fold_in(own_key, 6)
    for axis_at, shards_of in shards:
        steps = jnp.exp(jax.random.uniform(jax.random.fold_in(own, axis_at), (shards_of,), jnp.float32, low / len(shards), high / len(shards)))
        loudness = loudness * jnp.repeat(steps, shape[axis_at] // shards_of).reshape([-1 if axis == axis_at else 1 for axis in range(len(shape))])
    return loudness


def noise(key, extent, scale, bound, cuts=(), kind=jnp.bfloat16):
    values = jax.random.normal(key, extent, jnp.float32) * scale
    if len(cuts) > 0:
        values = block_levels(key, extent, cuts, -0.22, 0.18) * values
    return jnp.clip(values, min=-bound, max=bound).astype(kind)


def setup_inputs(seed: int = 0) -> dict:
    splits = jax.random.split(jax.random.key(seed), 11)
    orbital_ints = noise(splits[0], (ORBS, NAUX, NV), (NAUX // 16) ** -0.5, 1.5, ((0, 512),))
    pair_fock = jnp.clip(-2.0 + 1.8 * jax.random.uniform(splits[1], (PAIRS, 2), jnp.float32) ** block_levels(splits[1], (PAIRS, 2), ((0, 512),), -0.2, 0.2), -2.0, -0.2)
    pair_orbitals = draw_pair_orbitals(jax.random.fold_in(splits[10], 71), 0)
    rank_bucket = with_ends(jax.random.randint(splits[3], (PAIRS,), 1, 4), jax.random.fold_in(splits[3], 1), 1, 3).astype(jnp.int32)
    pno_coeffs = noise(splits[4], (PAIRS, NV, R), NV ** -0.5, 0.375, ((0, 512),))
    pno_energy = jnp.clip(jnp.exp(math.log(4.0) - 2.9957323 * jax.random.uniform(splits[5], (PAIRS, R), jnp.float32) ** block_levels(splits[5], (PAIRS, R), ((0, 512),), -0.2, 0.2)), 0.2, 4.0)
    amplitudes = noise(splits[6], (PAIRS, R, R), 0.3, 1.796875, ((0, 512),))
    neighbors = draw_neighbors(jax.random.fold_in(splits[10], 71), 0)
    intersections = noise(splits[8], (PAIRS, NB, R, R), 0.2, 1.1953125, ((0, 512),))
    coupling_fock = noise(splits[9], (PAIRS, NB), 1.0, 4.0, ((0, 512),), jnp.float32)
    return {"orbital_ints": orbital_ints, "pair_fock": pair_fock, "pair_orbitals": pair_orbitals, "rank_bucket": rank_bucket, "pno_coeffs": pno_coeffs, "pno_energy": pno_energy, "amplitudes": amplitudes, "neighbors": neighbors, "intersections": intersections, "coupling_fock": coupling_fock}


def reference(orbital_ints, pair_fock, pair_orbitals, rank_bucket, pno_coeffs, pno_energy, amplitudes, neighbors, intersections, coupling_fock):
    positions = jnp.arange(R, dtype=jnp.int32)
    live_rows = positions[None, :] < (rank_bucket * (R // 3)).astype(jnp.int32)[:, None]
    live_block = live_rows[:, :, None] & live_rows[:, None, :]
    masked_amplitudes = jnp.where(live_block, amplitudes, jnp.zeros_like(amplitudes))
    blocks_total = PAIRS // PAIR_DEV

    def by_block(whole_array):
        return whole_array.reshape((blocks_total, PAIR_DEV) + whole_array.shape[1:])

    def one_block(inputs):
        orbitals, fock_pair, coeffs, energy, amplitude_block, nearby, intersection, weights, live_pair = inputs
        coeffs_wide = coeffs.astype(jnp.float32)
        first_blocks = jnp.take(orbital_ints, orbitals[:, 0].astype(jnp.int32), axis=0).astype(jnp.float32)
        first_transformed = jnp.einsum("pqv,pvr->pqr", first_blocks, coeffs_wide).astype(jnp.bfloat16)
        second_blocks = jnp.take(orbital_ints, orbitals[:, 1].astype(jnp.int32), axis=0).astype(jnp.float32)
        second_transformed = jnp.einsum("pqv,pvr->pqr", second_blocks, coeffs_wide).astype(jnp.bfloat16)
        exchange_integrals = jnp.einsum("pqa,pqb->pab", first_transformed.astype(jnp.float32), second_transformed.astype(jnp.float32))
        energy_gap = energy[:, :, None] + energy[:, None, :] - (fock_pair[:, 0] + fock_pair[:, 1])[:, None, None]
        diagonal_term = energy_gap * amplitude_block.astype(jnp.float32)
        neighbor_amps = jnp.take(masked_amplitudes, nearby.astype(jnp.int32), axis=0).astype(jnp.float32)
        intersection_wide = intersection.astype(jnp.float32)
        half_coupled = jnp.einsum("pnac,pncd->pnad", intersection_wide, neighbor_amps).astype(jnp.bfloat16)
        coupled = jnp.einsum("pnad,pnbd->pnab", half_coupled.astype(jnp.float32), intersection_wide)
        coupling = jnp.sum(weights[:, :, None, None] * coupled, axis=1)
        total = exchange_integrals + diagonal_term - coupling
        return jnp.where(live_pair, total, jnp.zeros_like(total))

    pieces = tuple(by_block(item) for item in (pair_orbitals, pair_fock, pno_coeffs, pno_energy, amplitudes, neighbors, intersections, coupling_fock, live_block))
    result = lax.map(one_block, pieces)
    return result.reshape(PAIRS, R, R)
```

```python
import functools

import jax
import jax.numpy as jnp
from jax import lax
from jax.experimental import pallas as pl
from jax.experimental.pallas import tpu as pltpu
from jax.sharding import PartitionSpec as P

MESH = pl.DeviceIdType.MESH
BF16 = jnp.bfloat16
F32 = jnp.float32
NT = (((1,), (1,)), ((), ()))
NN = (((1,), (0,)), ((), ()))

GROUPS = 16
PEERS = 32
PAIRS = 32
R = 96
AUX = 256
SLOTS = 4
CHUNKS = 4
HALF = GROUPS // 2
ROWS = 2 * AUX // CHUNKS
STRIDE = 13
LANES = 128


def dot(a, b, dims):
    return lax.dot_general(a, b, dims, preferred_element_type=F32)


def shifted(device, k, sign):
    core, y, x = device % 2, device // 2 % 4, device // 8
    dc, dy, dx = k % 2, k // 2 % 4, k // 8
    return ((x + sign * dx + 4) % 4 * 4 + (y + sign * dy + 4) % 4) * 2 + (core + dc) % 2


def iota(shape, axis):
    return lax.broadcasted_iota(jnp.int32, shape, axis)


def as_column(row):
    n = row.shape[1]
    return jnp.sum(jnp.where(iota((n, n), 0) == iota((n, n), 1), row, 0), axis=1, keepdims=True)


def as_lanes(column):
    n = column.shape[0]
    return jnp.sum(jnp.where(iota((n, LANES), 0) == iota((n, LANES), 1), column, 0), axis=0, keepdims=True)


def scattered(slot, value):
    return jnp.sum(jnp.where(slot == iota((slot.shape[0], LANES), 1), value, 0), axis=0, keepdims=True)


def kernel(
    orb_hbm, coeffs_hbm, amps_hbm, inter_hbm, energy, orbitals, nearby, rank, fock, weight,
    out, orbs, coeffs, amps, masked, inter, first, exchange, coupled, outbox, inbox, asked, table,
    table_s, asked_s, local_sem, ring_out, ring_in, ask_out, ask_in, amp_out, amp_in,
):
    grp = lax.axis_index("grp")
    me = lax.axis_index("pair")
    right = lax.rem(grp + 1, GROUPS)
    left = lax.rem(grp + GROUPS - 1, GROUPS)

    own_orbs = pltpu.make_async_copy(orb_hbm, orbs.at[0], local_sem.at[0])
    own_coeffs = pltpu.make_async_copy(coeffs_hbm, coeffs, local_sem.at[1])
    own_amps = pltpu.make_async_copy(amps_hbm, amps, local_sem.at[2])
    own_inter = pltpu.make_async_copy(inter_hbm, inter, local_sem.at[3])
    own_orbs.start()

    barrier = pltpu.get_barrier_semaphore()
    for target in (right, left):
        pl.semaphore_signal(barrier, inc=1, device_id=(target, me), device_id_type=MESH)

    @pl.loop(1, PEERS)
    def _(k):
        pl.semaphore_signal(barrier, inc=1, device_id=(grp, shifted(me, k, 1)), device_id_type=MESH)

    own_amps.start()
    own_coeffs.start()
    own_inter.start()
    own_orbs.wait()
    pl.semaphore_wait(barrier, PEERS + 1)

    def ring(d, s, c):
        chunk = c if d == 0 else CHUNKS - 1 - c
        rows = pl.ds(chunk * ROWS, ROWS)
        here = (GROUPS - (s - 1)) % GROUPS if d == 0 else s - 1
        there = GROUPS - s if d == 0 else s
        return pltpu.make_async_remote_copy(
            orbs.at[here, rows], orbs.at[there, rows], ring_out.at[d, s - 1, c], ring_in.at[d, s - 1, c],
            device_id=(right if d == 0 else left, me), device_id_type=MESH,
        )

    def ask(k):
        return pltpu.make_async_remote_copy(
            table.at[pl.ds(0, 1)], asked.at[pl.ds(k, 1)], ask_out.at[k], ask_in.at[k],
            device_id=(grp, shifted(me, k, 1)), device_id_type=MESH,
        )

    def answer(k):
        return pltpu.make_async_remote_copy(
            outbox.at[k], inbox.at[k], amp_out.at[k], amp_in.at[k],
            device_id=(grp, shifted(me, k, -1)), device_id_type=MESH,
        )

    @pl.loop(0, CHUNKS)
    def _(c):
        ring(0, 1, c).start()
        ring(1, 1, c).start()

    above = iota((PAIRS, PAIRS), 1) < iota((PAIRS, PAIRS), 0)

    def same(column, row):
        return column == row

    def count(hits):
        return jnp.sum(jnp.where(hits, 1, 0), axis=1, keepdims=True)

    def within(place):
        return jnp.minimum(place, SLOTS - 1)

    column_of = (nearby[...] >> 5) & (PEERS - 1)
    core, y, x = me % 2, me // 2 % 4, me // 8
    distance = (((column_of >> 3) - x) & 3) * 8 + ((((column_of >> 1) & 3) - y) & 3) * 2 + ((column_of - core) & 1)
    at = nearby[...] & (PAIRS - 1)
    rows = [distance[0:1], distance[1:2]]
    columns = [as_column(r) for r in rows]
    wanted = [as_column(at[0:1]), as_column(at[1:2])]
    place = [
        columns[0] * SLOTS + within(count(same(columns[0], rows[0]) & above)),
        columns[1] * SLOTS + within(count(same(columns[1], rows[0])) + count(same(columns[1], rows[1]) & above)),
    ]
    pair = iota((PAIRS, 1), 0)
    table[0:1] = (scattered(place[0], wanted[0]) + scattered(place[1], wanted[1])) & (PAIRS - 1)

    @pl.loop(1, PEERS)
    def _(k):
        ask((k * STRIDE) % PEERS).start()

    table[1:2] = (scattered(place[0], 2 * pair) + scattered(place[1], 2 * pair + 1)) & (2 * PAIRS - 1)
    table[2:3] = as_lanes(place[0])
    table[3:4] = as_lanes(place[1])
    second = orbitals[1:2]
    home = ((second >> 6) - grp) & (GROUPS - 1)
    home_column = as_column(home)
    home_place = home_column * SLOTS + within(count(same(home_column, home) & above))
    table[4:5] = scattered(home_place, pair) & (PAIRS - 1)
    table[5:6] = scattered(home_place, as_column(second & 1))
    table[6:7] = as_lanes(home_place)
    table[7:8] = as_lanes(as_column(orbitals[0:1] & 1))
    to_scalar = pltpu.make_async_copy(table, table_s, local_sem.at[4])
    to_scalar.start()
    own_amps.wait()

    def live(p):
        top = rank[p] * (R // 3)
        return (iota((R, R), 0) < top) & (iota((R, R), 1) < top)

    def mask_pair(p, _):
        mine = amps[p].astype(F32)
        masked[p] = jnp.where(live(p), mine, 0.0).astype(BF16)
        return 0

    lax.fori_loop(0, PAIRS, mask_pair, 0, unroll=4)
    to_scalar.wait()
    own_coeffs.wait()

    def first_pair(p, _):
        half = table_s[7, p]
        block = jnp.where(half == 1, orbs[0, AUX:], orbs[0, :AUX])
        first[p] = dot(coeffs[p], block, NT).astype(BF16)
        return 0

    lax.fori_loop(0, PAIRS, first_pair, 0, unroll=4)

    @pl.loop(1, PEERS)
    def _(k):
        ask(k).wait_recv()

    asked_in = pltpu.make_async_copy(asked, asked_s, local_sem.at[5])
    asked_in.start()
    asked_in.wait()

    @pl.loop(1, PEERS)
    def _(i):
        k = (i * STRIDE) % PEERS
        blocks = [masked[asked_s[k, SLOTS * k + j]] for j in range(SLOTS)]
        for j in range(3):
            outbox[k, j] = jnp.concatenate([blocks[j], blocks[3][:, 32 * j : 32 * j + 32]], axis=1)
        answer(k).start()

    own_inter.wait()

    def exchange_slot(kz, j):
        slot = kz * SLOTS + j
        p, half = table_s[4, slot], table_s[5, slot]
        block = jnp.where(half == 1, orbs[kz, AUX:], orbs[kz, :AUX])
        moved = dot(coeffs[p], block, NT).astype(BF16)
        exchange[slot] = dot(first[p], moved, NT)

    def couple(slot, block):
        t = inter[table_s[1, slot]]
        coupled[slot] = dot(dot(t, block, NN).astype(BF16), t, NT)

    def couple_own():
        for j in range(SLOTS):
            couple(j, masked[table_s[0, j]])

    def couple_peer(k):
        answer(k).wait_recv()
        parts = [inbox[k, j] for j in range(3)]
        for j in range(3):
            couple(SLOTS * k + j, parts[j][:, :R])
        couple(SLOTS * k + 3, jnp.concatenate([part[:, R:] for part in parts], axis=1))

    def diagonal(p):
        across = energy[pl.ds(p, 1), :]
        down = jnp.sum(jnp.where(iota((R, R), 0) == iota((R, R), 1), across, 0.0), axis=1, keepdims=True)
        out[p] = (down + across - (fock[0, p] + fock[1, p])) * amps[p].astype(F32)

    def forward(s, c):
        for d in (0, 1):
            ring(d, s - 1, c).wait_recv()
            ring(d, s, c).start()

    def exchange_some(s, c):
        kz = jnp.where(c < 2, s, (GROUPS - s) % GROUPS)
        for j in range(2):
            exchange_slot(kz, c % 2 * 2 + j)

    @pl.loop(0, CHUNKS)
    def _(c):
        forward(2, c)
        exchange_some(0, c)

        @pl.loop(0, PAIRS // CHUNKS)
        def _(p):
            diagonal(c * (PAIRS // CHUNKS) + p)

    couple_own()
    per_unit = 1
    begin = 3

    @pl.loop(begin, HALF)
    def _(s):
        @pl.loop(0, CHUNKS)
        def _(c):
            forward(s, c)
            exchange_some(s - 2, c)
            couple_peer((((s - begin) * CHUNKS + c + 1) * STRIDE) % PEERS)

    done = 1 + (HALF - begin) * CHUNKS

    @pl.loop(0, 2)
    def _(c):
        forward(HALF, c)
        exchange_some(HALF - 2, c)

    @pl.loop(2, CHUNKS)
    def _(c):
        ring(0, HALF - 1, c).wait_recv()
        ring(1, HALF - 1, c).wait_recv()
        exchange_some(HALF - 2, c)

    @pl.loop(0, CHUNKS)
    def _(c):
        exchange_some(HALF - 1, c)

    @pl.loop(done, PEERS)
    def _(i):
        couple_peer((i * STRIDE) % PEERS)

    @pl.loop(0, 2)
    def _(c):
        ring(0, HALF, c).wait_recv()
        ring(1, HALF, c).wait_recv()

    for j in range(SLOTS):
        exchange_slot(HALF, j)

    def finish(p, _):
        near = weight[0, p] * coupled[table_s[2, p]] + weight[1, p] * coupled[table_s[3, p]]
        out[p] = jnp.where(live(p), out[p] + exchange[table_s[6, p]] - near, 0.0)
        return 0

    lax.fori_loop(0, PAIRS, finish, 0, unroll=4)

    @pl.loop(1, PEERS)
    def _(k):
        ask(k).wait_send()
        answer(k).wait_send()

    @pl.loop(1, HALF)
    def _(s):
        @pl.loop(0, CHUNKS)
        def _(c):
            ring(0, s, c).wait_send()
            ring(1, s, c).wait_send()

    @pl.loop(0, 2)
    def _(c):
        ring(0, HALF, c).wait_send()
        ring(1, HALF, c).wait_send()


def local(
    orbital_ints, pair_fock, pair_orbitals, rank_bucket, pno_coeffs, pno_energy, amplitudes, neighbors, intersections, coupling_fock
):
    far = pl.BlockSpec(memory_space=pltpu.HBM)
    vector = pl.BlockSpec(memory_space=pltpu.VMEM)
    scalar = pl.BlockSpec(memory_space=pltpu.SMEM)
    dma = pltpu.SemaphoreType.DMA
    return pl.pallas_call(
        kernel,
        out_shape=jax.ShapeDtypeStruct((PAIRS, R, R), F32),
        in_specs=[far, far, far, far, vector, vector, vector, scalar, scalar, scalar],
        out_specs=vector,
        scratch_shapes=[
            pltpu.VMEM((GROUPS, 2 * AUX, AUX), BF16),
            pltpu.VMEM((PAIRS, R, AUX), BF16),
            pltpu.VMEM((PAIRS, R, R), BF16),
            pltpu.VMEM((PAIRS, R, R), BF16),
            pltpu.VMEM((2 * PAIRS, R, R), BF16),
            pltpu.VMEM((PAIRS, R, AUX), BF16),
            pltpu.VMEM((GROUPS * SLOTS, R, R), F32),
            pltpu.VMEM((PEERS * SLOTS, R, R), F32),
            pltpu.VMEM((PEERS, 3, R, LANES), BF16),
            pltpu.VMEM((PEERS, 3, R, LANES), BF16),
            pltpu.VMEM((PEERS, LANES), jnp.int32),
            pltpu.VMEM((8, LANES), jnp.int32),
            pltpu.SMEM((8, LANES), jnp.int32),
            pltpu.SMEM((PEERS, LANES), jnp.int32),
            dma((6,)),
            dma((2, HALF, CHUNKS)),
            dma((2, HALF, CHUNKS)),
            dma((PEERS,)),
            dma((PEERS,)),
            dma((PEERS,)),
            dma((PEERS,)),
        ],
        compiler_params=pltpu.CompilerParams(
            collective_id=0, has_side_effects=True, vmem_limit_bytes=48 * 2**20
        ),
    )(
        orbital_ints.reshape(2 * AUX, AUX),
        jnp.swapaxes(pno_coeffs, 1, 2),
        amplitudes,
        intersections.reshape(2 * PAIRS, R, R),
        pno_energy,
        pair_orbitals.T,
        neighbors.T,
        rank_bucket,
        pair_fock.T,
        coupling_fock.T,
    )


def solution(mesh):
    rows = P(("grp", "pair"))
    return jax.shard_map(
        local,
        mesh=mesh,
        in_specs=(rows,) * 10,
        out_specs=rows,
        check_vma=False,
    )
```

```python
import functools

import jax
import jax.numpy as jnp
from jax import lax
from jax.experimental import pallas as pl
from jax.experimental.pallas import tpu as pltpu
from jax.sharding import PartitionSpec as P

MESH = pl.DeviceIdType.MESH
BF16 = jnp.bfloat16
F32 = jnp.float32
NT = (((1,), (1,)), ((), ()))
NN = (((1,), (0,)), ((), ()))

GROUPS = 16
PEERS = 32
PAIRS = 32
R = 96
AUX = 256
SLOTS = 4
CHUNKS = 4
HALF = GROUPS // 2
ROWS = 2 * AUX // CHUNKS
STRIDE = 13
LANES = 128
ASK_AT = 2
PLAN = ((3, 6, 0), (6, 8, 4))
LAST = 4


def dot(a, b, dims):
    return lax.dot_general(a, b, dims, preferred_element_type=F32)


def shifted(device, k, sign):
    core, y, x = device % 2, device // 2 % 4, device // 8
    dc, dy, dx = k % 2, k // 2 % 4, k // 8
    return ((x + sign * dx + 4) % 4 * 4 + (y + sign * dy + 4) % 4) * 2 + (core + dc) % 2


def plane_of(device):
    core, y, x = device % 2, device // 2 % 4, device // 8
    xs = [(x + d) % 4 * 8 for d in range(4)]
    ys = [(y + d) % 4 * 2 for d in range(4)]
    return [xs[k // 8] + ys[k // 2 % 4] + (core + k % 2) % 2 for k in range(PEERS)]


def iota(shape, axis):
    return lax.broadcasted_iota(jnp.int32, shape, axis)


def as_column(row):
    n = row.shape[1]
    return jnp.sum(jnp.where(iota((n, n), 0) == iota((n, n), 1), row, 0), axis=1, keepdims=True)


def as_lanes(column):
    n = column.shape[0]
    return jnp.sum(jnp.where(iota((n, LANES), 0) == iota((n, LANES), 1), column, 0), axis=0, keepdims=True)


def scattered(slot, value):
    return jnp.sum(jnp.where(slot == iota((slot.shape[0], LANES), 1), value, 0), axis=0, keepdims=True)


def kernel(
    orb_hbm, coeffs_hbm, amps_hbm, inter_hbm, energy_hbm, orbitals_hbm, nearby_hbm, rank_hbm, fock_hbm, weight_hbm,
    out, orbs, coeffs, amps, masked, inter, energy, orbitals, nearby, rank, fock, weight,
    first, exchange, coupled, outbox, inbox, asked, table, table_s, asked_s, local_sem, ring_out, ring_in, ask_out, ask_in, amp_out, amp_in,
):
    grp = lax.axis_index("grp")
    me = lax.axis_index("pair")
    right = lax.rem(grp + 1, GROUPS)
    left = lax.rem(grp + GROUPS - 1, GROUPS)

    def load(i, source, target):
        copy = pltpu.make_async_copy(source, target, local_sem.at[i])
        copy.start()
        return copy

    own_orbs = load(0, orb_hbm, orbs.at[0])
    own_nearby = load(1, nearby_hbm, nearby)
    own_orbitals = load(2, orbitals_hbm, orbitals)
    own_rank = load(3, rank_hbm, rank)

    barrier = pltpu.get_barrier_semaphore()
    for target in (right, left):
        pl.semaphore_signal(barrier, inc=1, device_id=(target, me), device_id_type=MESH)

    plane = plane_of(me)
    for k in range(1, PEERS):
        pl.semaphore_signal(barrier, inc=1, device_id=(grp, plane[k]), device_id_type=MESH)

    own_amps = load(4, amps_hbm, amps)
    own_coeffs = load(5, coeffs_hbm, coeffs)
    own_inter = load(6, inter_hbm, inter)
    own_energy = load(7, energy_hbm, energy)
    own_fock = load(8, fock_hbm, fock)
    own_weight = load(9, weight_hbm, weight)
    own_orbs.wait()
    own_nearby.wait()
    own_orbitals.wait()
    pl.semaphore_wait(barrier, PEERS + 1)

    def ring(d, s, c):
        chunk = c if d == 0 else CHUNKS - 1 - c
        rows = pl.ds(chunk * ROWS, ROWS)
        here = (GROUPS - (s - 1)) % GROUPS if d == 0 else s - 1
        there = GROUPS - s if d == 0 else s
        return pltpu.make_async_remote_copy(
            orbs.at[here, rows], orbs.at[there, rows], ring_out.at[d, s - 1, c], ring_in.at[d, s - 1, c],
            device_id=(right if d == 0 else left, me), device_id_type=MESH,
        )

    def ask(k):
        return pltpu.make_async_remote_copy(
            table.at[pl.ds(0, 1)], asked.at[pl.ds(k, 1)], ask_out.at[k], ask_in.at[k],
            device_id=(grp, plane[k] if isinstance(k, int) else shifted(me, k, 1)), device_id_type=MESH,
        )

    def answer(k):
        return pltpu.make_async_remote_copy(
            outbox.at[k], inbox.at[k], amp_out.at[k], amp_in.at[k],
            device_id=(grp, shifted(me, k, -1)), device_id_type=MESH,
        )

    @pl.loop(0, CHUNKS)
    def _(c):
        ring(0, 1, c).start()
        ring(1, 1, c).start()

    above = iota((PAIRS, PAIRS), 1) < iota((PAIRS, PAIRS), 0)

    def same(column, row):
        return column == row

    def count(hits):
        return jnp.sum(jnp.where(hits, 1, 0), axis=1, keepdims=True)

    def within(place):
        return jnp.minimum(place, SLOTS - 1)

    column_of = (nearby[...] >> 5) & (PEERS - 1)
    core, y, x = me % 2, me // 2 % 4, me // 8
    distance = (((column_of >> 3) - x) & 3) * 8 + ((((column_of >> 1) & 3) - y) & 3) * 2 + ((column_of - core) & 1)
    at = nearby[...] & (PAIRS - 1)
    rows = [distance[0:1], distance[1:2]]
    columns = [as_column(r) for r in rows]
    wanted = [as_column(at[0:1]), as_column(at[1:2])]
    place = [
        columns[0] * SLOTS + within(count(same(columns[0], rows[0]) & above)),
        columns[1] * SLOTS + within(count(same(columns[1], rows[0])) + count(same(columns[1], rows[1]) & above)),
    ]
    pair = iota((PAIRS, 1), 0)
    table[0:1] = (scattered(place[0], wanted[0]) + scattered(place[1], wanted[1])) & (PAIRS - 1)

    for k in range(1, PEERS):
        ask((k * STRIDE) % PEERS).start()

    table[1:2] = (scattered(place[0], 2 * pair) + scattered(place[1], 2 * pair + 1)) & (2 * PAIRS - 1)
    table[2:3] = as_lanes(place[0])
    table[3:4] = as_lanes(place[1])
    second = orbitals[1:2]
    home = ((second >> 6) - grp) & (GROUPS - 1)
    home_column = as_column(home)
    home_place = home_column * SLOTS + within(count(same(home_column, home) & above))
    table[4:5] = scattered(home_place, pair) & (PAIRS - 1)
    table[5:6] = scattered(home_place, as_column(second & 1))
    table[6:7] = as_lanes(home_place)
    table[7:8] = as_lanes(as_column(orbitals[0:1] & 1))
    to_scalar = load(10, table, table_s)
    own_amps.wait()
    own_rank.wait()

    def live(p):
        top = rank[p] * (R // 3)
        return (iota((R, R), 0) < top) & (iota((R, R), 1) < top)

    def mask_pair(p, _):
        mine = amps[p].astype(F32)
        masked[p] = jnp.where(live(p), mine, 0.0).astype(BF16)
        return 0

    lax.fori_loop(0, PAIRS, mask_pair, 0, unroll=4)
    to_scalar.wait()
    own_coeffs.wait()

    def first_pair(p, _):
        half = table_s[7, p]
        block = jnp.where(half == 1, orbs[0, AUX:], orbs[0, :AUX])
        first[p] = dot(coeffs[p], block, NT).astype(BF16)
        return 0

    lax.fori_loop(0, PAIRS, first_pair, 0, unroll=4)

    def forward(s, c):
        for d in (0, 1):
            ring(d, s - 1, c).wait_recv()
            ring(d, s, c).start()

    @pl.loop(0, ASK_AT)
    def _(c):
        forward(2, c)

    @pl.loop(1, PEERS)
    def _(k):
        ask(k).wait_recv()

    load(11, asked, asked_s).wait()

    @pl.loop(1, PEERS)
    def _(i):
        k = (i * STRIDE) % PEERS
        blocks = [masked[asked_s[k, SLOTS * k + j]] for j in range(SLOTS)]
        for j in range(3):
            outbox[k, j] = jnp.concatenate([blocks[j], blocks[3][:, 32 * j : 32 * j + 32]], axis=1)
        answer(k).start()

    @pl.loop(ASK_AT, CHUNKS)
    def _(c):
        forward(2, c)

    own_inter.wait()
    own_energy.wait()
    own_fock.wait()
    own_weight.wait()

    def exchange_block(kz):
        slots = [kz * SLOTS + j for j in range(SLOTS)]
        pairs = [table_s[4, slot] for slot in slots]
        halves = [table_s[5, slot] for slot in slots]
        moved = [
            dot(coeffs[p], jnp.where(half == 1, orbs[kz, AUX:], orbs[kz, :AUX]), NT).astype(BF16)
            for p, half in zip(pairs, halves)
        ]
        sums = [dot(first[p], m, NT) for p, m in zip(pairs, moved)]
        for slot, total in zip(slots, sums):
            exchange[slot] = total

    def couple(slots, blocks):
        turns = [inter[table_s[1, slot]] for slot in slots]
        halves = [dot(t, block, NN).astype(BF16) for t, block in zip(turns, blocks)]
        sums = [dot(half, t, NT) for half, t in zip(halves, turns)]
        for slot, total in zip(slots, sums):
            coupled[slot] = total

    def couple_own():
        couple(range(SLOTS), [masked[table_s[0, j]] for j in range(SLOTS)])

    def couple_peers(begin, n):
        slots, blocks = [], []
        for i in range(n):
            k = ((begin + i) * STRIDE) % PEERS
            answer(k).wait_recv()
            parts = [inbox[k, j] for j in range(3)]
            slots += [SLOTS * k + j for j in range(SLOTS)]
            blocks += [part[:, :R] for part in parts]
            blocks.append(jnp.concatenate([part[:, R:] for part in parts], axis=1))
        if n:
            couple(slots, blocks)

    def diagonal(p, _):
        across = energy[pl.ds(p, 1), :]
        down = jnp.sum(jnp.where(iota((R, R), 0) == iota((R, R), 1), across, 0.0), axis=1, keepdims=True)
        out[p] = (down + across - (fock[0, p] + fock[1, p])) * amps[p].astype(F32)
        return 0

    def exchange_side(s, side):
        exchange_block(jnp.where(side == 0, s, GROUPS - s))

    done = 1
    for low, high, n in PLAN:
        begin = done

        @pl.loop(low, high)
        def _(s):
            @pl.loop(0, 2)
            def _(h):
                forward(s, 2 * h)
                exchange_side(s - 2, h)
                forward(s, 2 * h + 1)
                couple_peers(begin + (2 * (s - low) + h) * n, n)

        done += (high - low) * 2 * n

        if low == 3:
            exchange_block(0)
            couple_own()
            lax.fori_loop(0, PAIRS, diagonal, 0, unroll=4)

    forward(HALF, 0)
    forward(HALF, 1)
    exchange_side(HALF - 2, 0)
    exchange_side(HALF - 2, 1)
    couple_peers(done, LAST)
    done += LAST

    for c in (2, 3):
        for d in (0, 1):
            ring(d, HALF - 1, c).wait_recv()

    @pl.loop(0, 2)
    def _(h):
        exchange_side(HALF - 1, h)

    @pl.loop(0, (PEERS - done) // 2)
    def _(i):
        couple_peers(done + 2 * i, 2)

    couple_peers(done + (PEERS - done) // 2 * 2, (PEERS - done) % 2)

    @pl.loop(0, 2)
    def _(c):
        ring(0, HALF, c).wait_recv()
        ring(1, HALF, c).wait_recv()

    exchange_block(HALF)

    def finish(p, _):
        near = weight[0, p] * coupled[table_s[2, p]] + weight[1, p] * coupled[table_s[3, p]]
        out[p] = jnp.where(live(p), out[p] + exchange[table_s[6, p]] - near, 0.0)
        return 0

    lax.fori_loop(0, PAIRS, finish, 0, unroll=4)

    @pl.loop(1, PEERS)
    def _(k):
        ask(k).wait_send()
        answer(k).wait_send()

    @pl.loop(1, HALF)
    def _(s):
        @pl.loop(0, CHUNKS)
        def _(c):
            ring(0, s, c).wait_send()
            ring(1, s, c).wait_send()

    @pl.loop(0, 2)
    def _(c):
        ring(0, HALF, c).wait_send()
        ring(1, HALF, c).wait_send()


def local(
    orbital_ints, pair_fock, pair_orbitals, rank_bucket, pno_coeffs, pno_energy, amplitudes, neighbors, intersections, coupling_fock
):
    dma = pltpu.SemaphoreType.DMA
    return pl.pallas_call(
        kernel,
        out_shape=jax.ShapeDtypeStruct((PAIRS, R, R), F32),
        in_specs=[pl.BlockSpec(memory_space=pltpu.HBM)] * 10,
        out_specs=pl.BlockSpec(memory_space=pltpu.VMEM),
        scratch_shapes=[
            pltpu.VMEM((GROUPS, 2 * AUX, AUX), BF16),
            pltpu.VMEM((PAIRS, R, AUX), BF16),
            pltpu.VMEM((PAIRS, R, R), BF16),
            pltpu.VMEM((PAIRS, R, R), BF16),
            pltpu.VMEM((2 * PAIRS, R, R), BF16),
            pltpu.VMEM((PAIRS, R), F32),
            pltpu.VMEM((2, PAIRS), jnp.int32),
            pltpu.VMEM((2, PAIRS), jnp.int32),
            pltpu.SMEM((PAIRS,), jnp.int32),
            pltpu.SMEM((2, PAIRS), F32),
            pltpu.SMEM((2, PAIRS), F32),
            pltpu.VMEM((PAIRS, R, AUX), BF16),
            pltpu.VMEM((GROUPS * SLOTS, R, R), F32),
            pltpu.VMEM((PEERS * SLOTS, R, R), F32),
            pltpu.VMEM((PEERS, 3, R, LANES), BF16),
            pltpu.VMEM((PEERS, 3, R, LANES), BF16),
            pltpu.VMEM((PEERS, LANES), jnp.int32),
            pltpu.VMEM((8, LANES), jnp.int32),
            pltpu.SMEM((8, LANES), jnp.int32),
            pltpu.SMEM((PEERS, LANES), jnp.int32),
            dma((12,)),
            dma((2, HALF, CHUNKS)),
            dma((2, HALF, CHUNKS)),
            dma((PEERS,)),
            dma((PEERS,)),
            dma((PEERS,)),
            dma((PEERS,)),
        ],
        compiler_params=pltpu.CompilerParams(
            collective_id=0, has_side_effects=True, vmem_limit_bytes=63 * 2**20
        ),
    )(
        orbital_ints.reshape(2 * AUX, AUX),
        jnp.swapaxes(pno_coeffs, 1, 2),
        amplitudes,
        intersections.reshape(2 * PAIRS, R, R),
        pno_energy,
        pair_orbitals.T,
        neighbors.T,
        rank_bucket,
        pair_fock.T,
        coupling_fock.T,
    )


def solution(mesh):
    rows = P(("grp", "pair"))
    return jax.shard_map(
        local,
        mesh=mesh,
        in_specs=(rows,) * 10,
        out_specs=rows,
        check_vma=False,
    )
```

```python
import functools

import jax
import jax.numpy as jnp
from jax import lax
from jax.experimental import pallas as pl
from jax.experimental.pallas import tpu as pltpu
from jax.sharding import PartitionSpec as P

MESH = pl.DeviceIdType.MESH
BF16 = jnp.bfloat16
F32 = jnp.float32
NT = (((1,), (1,)), ((), ()))
NN = (((1,), (0,)), ((), ()))

GROUPS = 16
PEERS = 32
PAIRS = 32
R = 96
AUX = 256
SLOTS = 4
CHUNKS = 4
HALF = GROUPS // 2
ROWS = 2 * AUX // CHUNKS
STRIDE = 13
LANES = 128
ASK_AT = 2
PLAN = ((3, 6, 0), (6, 7, 3), (7, 8, 6))
LAST = 6


def dot(a, b, dims):
    return lax.dot_general(a, b, dims, preferred_element_type=F32)


def shifted(device, k, sign):
    core, y, x = device % 2, device // 2 % 4, device // 8
    dc, dy, dx = k % 2, k // 2 % 4, k // 8
    return ((x + sign * dx + 4) % 4 * 4 + (y + sign * dy + 4) % 4) * 2 + (core + dc) % 2


def plane_of(device):
    core, y, x = device % 2, device // 2 % 4, device // 8
    xs = [(x + d) % 4 * 8 for d in range(4)]
    ys = [(y + d) % 4 * 2 for d in range(4)]
    return [xs[k // 8] + ys[k // 2 % 4] + (core + k % 2) % 2 for k in range(PEERS)]


def iota(shape, axis):
    return lax.broadcasted_iota(jnp.int32, shape, axis)


def as_column(row):
    n = row.shape[1]
    return jnp.sum(jnp.where(iota((n, n), 0) == iota((n, n), 1), row, 0), axis=1, keepdims=True)


def as_lanes(column):
    n = column.shape[0]
    return jnp.sum(jnp.where(iota((n, LANES), 0) == iota((n, LANES), 1), column, 0), axis=0, keepdims=True)


def scattered(slot, value):
    return jnp.sum(jnp.where(slot == iota((slot.shape[0], LANES), 1), value, 0), axis=0, keepdims=True)


def kernel(
    orb_hbm, coeffs_hbm, amps_hbm, inter_hbm, energy_hbm, orbitals_hbm, nearby_hbm, rank_hbm, fock_hbm, weight_hbm,
    out, orbs, coeffs, amps, masked, inter, energy, orbitals, nearby, rank, fock, weight,
    first, exchange, coupled, outbox, inbox, asked, table, table_s, asked_s, local_sem, ring_out, ring_in, ask_out, ask_in, amp_out, amp_in,
):
    grp = lax.axis_index("grp")
    me = lax.axis_index("pair")
    right = lax.rem(grp + 1, GROUPS)
    left = lax.rem(grp + GROUPS - 1, GROUPS)

    def load(i, source, target):
        copy = pltpu.make_async_copy(source, target, local_sem.at[i])
        copy.start()
        return copy

    own_orbs = load(0, orb_hbm, orbs.at[0])
    own_nearby = load(1, nearby_hbm, nearby)
    own_orbitals = load(2, orbitals_hbm, orbitals)
    own_rank = load(3, rank_hbm, rank)

    barrier = pltpu.get_barrier_semaphore()
    for target in (right, left):
        pl.semaphore_signal(barrier, inc=1, device_id=(target, me), device_id_type=MESH)

    plane = plane_of(me)
    for k in range(1, PEERS):
        pl.semaphore_signal(barrier, inc=1, device_id=(grp, plane[k]), device_id_type=MESH)

    own_amps = load(4, amps_hbm, amps)
    own_coeffs = load(5, coeffs_hbm, coeffs)
    own_inter = load(6, inter_hbm, inter)
    own_energy = load(7, energy_hbm, energy)
    own_fock = load(8, fock_hbm, fock)
    own_weight = load(9, weight_hbm, weight)
    own_orbs.wait()
    own_nearby.wait()
    own_orbitals.wait()
    pl.semaphore_wait(barrier, PEERS + 1)

    def ring(d, s, c):
        chunk = c if d == 0 else CHUNKS - 1 - c
        rows = pl.ds(chunk * ROWS, ROWS)
        here = (GROUPS - (s - 1)) % GROUPS if d == 0 else s - 1
        there = GROUPS - s if d == 0 else s
        return pltpu.make_async_remote_copy(
            orbs.at[here, rows], orbs.at[there, rows], ring_out.at[d, s - 1, c], ring_in.at[d, s - 1, c],
            device_id=(right if d == 0 else left, me), device_id_type=MESH,
        )

    def ask(k):
        return pltpu.make_async_remote_copy(
            table.at[pl.ds(0, 1)], asked.at[pl.ds(k, 1)], ask_out.at[k], ask_in.at[k],
            device_id=(grp, plane[k] if isinstance(k, int) else shifted(me, k, 1)), device_id_type=MESH,
        )

    def answer(k):
        return pltpu.make_async_remote_copy(
            outbox.at[k], inbox.at[k], amp_out.at[k], amp_in.at[k],
            device_id=(grp, shifted(me, k, -1)), device_id_type=MESH,
        )

    @pl.loop(0, CHUNKS)
    def _(c):
        ring(0, 1, c).start()
        ring(1, 1, c).start()

    above = iota((PAIRS, PAIRS), 1) < iota((PAIRS, PAIRS), 0)

    def same(column, row):
        return column == row

    def count(hits):
        return jnp.sum(jnp.where(hits, 1, 0), axis=1, keepdims=True)

    def within(place):
        return jnp.minimum(place, SLOTS - 1)

    column_of = (nearby[...] >> 5) & (PEERS - 1)
    core, y, x = me % 2, me // 2 % 4, me // 8
    distance = (((column_of >> 3) - x) & 3) * 8 + ((((column_of >> 1) & 3) - y) & 3) * 2 + ((column_of - core) & 1)
    at = nearby[...] & (PAIRS - 1)
    rows = [distance[0:1], distance[1:2]]
    columns = [as_column(r) for r in rows]
    wanted = [as_column(at[0:1]), as_column(at[1:2])]
    place = [
        columns[0] * SLOTS + within(count(same(columns[0], rows[0]) & above)),
        columns[1] * SLOTS + within(count(same(columns[1], rows[0])) + count(same(columns[1], rows[1]) & above)),
    ]
    pair = iota((PAIRS, 1), 0)
    table[0:1] = (scattered(place[0], wanted[0]) + scattered(place[1], wanted[1])) & (PAIRS - 1)

    for k in range(1, PEERS):
        ask((k * STRIDE) % PEERS).start()

    table[1:2] = (scattered(place[0], 2 * pair) + scattered(place[1], 2 * pair + 1)) & (2 * PAIRS - 1)
    table[2:3] = as_lanes(place[0])
    table[3:4] = as_lanes(place[1])
    second = orbitals[1:2]
    home = ((second >> 6) - grp) & (GROUPS - 1)
    home_column = as_column(home)
    home_place = home_column * SLOTS + within(count(same(home_column, home) & above))
    table[4:5] = scattered(home_place, pair) & (PAIRS - 1)
    table[5:6] = scattered(home_place, as_column(second & 1))
    table[6:7] = as_lanes(home_place)
    table[7:8] = as_lanes(as_column(orbitals[0:1] & 1))
    to_scalar = load(10, table, table_s)
    own_amps.wait()
    own_rank.wait()

    def live(p):
        top = rank[p] * (R // 3)
        return (iota((R, R), 0) < top) & (iota((R, R), 1) < top)

    def mask_pair(p, _):
        mine = amps[p].astype(F32)
        masked[p] = jnp.where(live(p), mine, 0.0).astype(BF16)
        return 0

    lax.fori_loop(0, PAIRS, mask_pair, 0, unroll=4)
    to_scalar.wait()
    own_coeffs.wait()

    def first_pair(p, _):
        half = table_s[7, p]
        block = jnp.where(half == 1, orbs[0, AUX:], orbs[0, :AUX])
        first[p] = dot(coeffs[p], block, NT).astype(BF16)
        return 0

    lax.fori_loop(0, PAIRS, first_pair, 0, unroll=4)

    def forward(s, c):
        for d in (0, 1):
            ring(d, s - 1, c).wait_recv()
            ring(d, s, c).start()

    @pl.loop(0, ASK_AT)
    def _(c):
        forward(2, c)

    @pl.loop(1, PEERS)
    def _(k):
        ask(k).wait_recv()

    load(11, asked, asked_s).wait()

    @pl.loop(1, PEERS)
    def _(i):
        k = (i * STRIDE) % PEERS
        blocks = [masked[asked_s[k, SLOTS * k + j]] for j in range(SLOTS)]
        for j in range(3):
            outbox[k, j] = jnp.concatenate([blocks[j], blocks[3][:, 32 * j : 32 * j + 32]], axis=1)
        answer(k).start()

    @pl.loop(ASK_AT, CHUNKS)
    def _(c):
        forward(2, c)

    own_inter.wait()
    own_energy.wait()
    own_fock.wait()
    own_weight.wait()

    def exchange_block(kz):
        slots = [kz * SLOTS + j for j in range(SLOTS)]
        pairs = [table_s[4, slot] for slot in slots]
        halves = [table_s[5, slot] for slot in slots]
        moved = [
            dot(coeffs[p], jnp.where(half == 1, orbs[kz, AUX:], orbs[kz, :AUX]), NT).astype(BF16)
            for p, half in zip(pairs, halves)
        ]
        sums = [dot(first[p], m, NT) for p, m in zip(pairs, moved)]
        for slot, total in zip(slots, sums):
            exchange[slot] = total

    def couple(slots, blocks):
        turns = [inter[table_s[1, slot]] for slot in slots]
        halves = [dot(t, block, NN).astype(BF16) for t, block in zip(turns, blocks)]
        sums = [dot(half, t, NT) for half, t in zip(halves, turns)]
        for slot, total in zip(slots, sums):
            coupled[slot] = total

    def couple_own():
        couple(range(SLOTS), [masked[table_s[0, j]] for j in range(SLOTS)])

    def couple_peers(begin, n):
        slots, blocks = [], []
        for i in range(n):
            k = ((begin + i) * STRIDE) % PEERS
            answer(k).wait_recv()
            parts = [inbox[k, j] for j in range(3)]
            slots += [SLOTS * k + j for j in range(SLOTS)]
            blocks += [part[:, :R] for part in parts]
            blocks.append(jnp.concatenate([part[:, R:] for part in parts], axis=1))
        if n:
            couple(slots, blocks)

    def diagonal(p, _):
        across = energy[pl.ds(p, 1), :]
        down = jnp.sum(jnp.where(iota((R, R), 0) == iota((R, R), 1), across, 0.0), axis=1, keepdims=True)
        out[p] = (down + across - (fock[0, p] + fock[1, p])) * amps[p].astype(F32)
        return 0

    def exchange_side(s, side):
        exchange_block(jnp.where(side == 0, s, GROUPS - s))

    done = 1
    for low, high, n in PLAN:
        begin = done

        @pl.loop(low, high)
        def _(s):
            @pl.loop(0, 2)
            def _(h):
                forward(s, 2 * h)
                exchange_side(s - 2, h)
                forward(s, 2 * h + 1)
                couple_peers(begin + (2 * (s - low) + h) * n, n)

        done += (high - low) * 2 * n

        if low == 3:
            exchange_block(0)
            couple_own()
            lax.fori_loop(0, PAIRS, diagonal, 0, unroll=4)

    forward(HALF, 0)
    forward(HALF, 1)
    exchange_side(HALF - 2, 0)
    exchange_side(HALF - 2, 1)
    couple_peers(done, LAST)
    done += LAST

    for c in (2, 3):
        for d in (0, 1):
            ring(d, HALF - 1, c).wait_recv()

    @pl.loop(0, 2)
    def _(h):
        exchange_side(HALF - 1, h)

    @pl.loop(0, (PEERS - done) // 2)
    def _(i):
        couple_peers(done + 2 * i, 2)

    couple_peers(done + (PEERS - done) // 2 * 2, (PEERS - done) % 2)

    @pl.loop(0, 2)
    def _(c):
        ring(0, HALF, c).wait_recv()
        ring(1, HALF, c).wait_recv()

    exchange_block(HALF)

    def finish(p, _):
        near = weight[0, p] * coupled[table_s[2, p]] + weight[1, p] * coupled[table_s[3, p]]
        out[p] = jnp.where(live(p), out[p] + exchange[table_s[6, p]] - near, 0.0)
        return 0

    lax.fori_loop(0, PAIRS, finish, 0, unroll=4)

    @pl.loop(1, PEERS)
    def _(k):
        ask(k).wait_send()
        answer(k).wait_send()

    @pl.loop(1, HALF)
    def _(s):
        @pl.loop(0, CHUNKS)
        def _(c):
            ring(0, s, c).wait_send()
            ring(1, s, c).wait_send()

    @pl.loop(0, 2)
    def _(c):
        ring(0, HALF, c).wait_send()
        ring(1, HALF, c).wait_send()


def local(
    orbital_ints, pair_fock, pair_orbitals, rank_bucket, pno_coeffs, pno_energy, amplitudes, neighbors, intersections, coupling_fock
):
    operands = (
        orbital_ints.reshape(2 * AUX, AUX),
        jnp.swapaxes(pno_coeffs, 1, 2),
        amplitudes,
        intersections.reshape(2 * PAIRS, R, R),
        pno_energy,
        pair_orbitals.T,
        neighbors.T,
        rank_bucket,
        pair_fock.T,
        coupling_fock.T,
    )
    dma = pltpu.SemaphoreType.DMA
    return pl.pallas_call(
        kernel,
        out_shape=pltpu.VMEM((PAIRS, R, R), F32),
        in_specs=[pl.BlockSpec(memory_space=pltpu.HBM)] * 10,
        out_specs=pl.BlockSpec(memory_space=pltpu.VMEM),
        scratch_shapes=[
            pltpu.VMEM((GROUPS, 2 * AUX, AUX), BF16),
            pltpu.VMEM((PAIRS, R, AUX), BF16),
            pltpu.VMEM((PAIRS, R, R), BF16),
            pltpu.VMEM((PAIRS, R, R), BF16),
            pltpu.VMEM((2 * PAIRS, R, R), BF16),
            pltpu.VMEM((PAIRS, R), F32),
            pltpu.VMEM((2, PAIRS), jnp.int32),
            pltpu.VMEM((2, PAIRS), jnp.int32),
            pltpu.SMEM((PAIRS,), jnp.int32),
            pltpu.SMEM((2, PAIRS), F32),
            pltpu.SMEM((2, PAIRS), F32),
            pltpu.VMEM((PAIRS, R, AUX), BF16),
            pltpu.VMEM((GROUPS * SLOTS, R, R), F32),
            pltpu.VMEM((PEERS * SLOTS, R, R), F32),
            pltpu.VMEM((PEERS, 3, R, LANES), BF16),
            pltpu.VMEM((PEERS, 3, R, LANES), BF16),
            pltpu.VMEM((PEERS, LANES), jnp.int32),
            pltpu.VMEM((8, LANES), jnp.int32),
            pltpu.SMEM((8, LANES), jnp.int32),
            pltpu.SMEM((PEERS, LANES), jnp.int32),
            dma((12,)),
            dma((2, HALF, CHUNKS)),
            dma((2, HALF, CHUNKS)),
            dma((PEERS,)),
            dma((PEERS,)),
            dma((PEERS,)),
            dma((PEERS,)),
        ],
        compiler_params=pltpu.CompilerParams(
            collective_id=0, has_side_effects=True, vmem_limit_bytes=48 * 2**20
        ),
    )(*[pltpu.with_memory_space_constraint(operand, pltpu.HBM) for operand in operands])


def solution(mesh):
    rows = P(("grp", "pair"))
    return jax.shard_map(
        local,
        mesh=mesh,
        in_specs=(rows,) * 10,
        out_specs=rows,
        check_vma=False,
    )
```

```python
import functools

import jax
import jax.numpy as jnp
from jax import lax
from jax.experimental import pallas as pl
from jax.experimental.pallas import tpu as pltpu
from jax.sharding import PartitionSpec as P

MESH = pl.DeviceIdType.MESH
BF16 = jnp.bfloat16
F32 = jnp.float32
NT = (((1,), (1,)), ((), ()))
NN = (((1,), (0,)), ((), ()))

GROUPS = 16
PEERS = 32
PAIRS = 32
R = 96
AUX = 256
SLOTS = 4
CHUNKS = 4
HALF = GROUPS // 2
ROWS = 2 * AUX // CHUNKS
STRIDE = 13
LANES = 128
ASK_AT = 2
PLAN = ((3, 6, 0), (6, 7, 3), (7, 8, 6))
LAST = 6


def dot(a, b, dims):
    return lax.dot_general(a, b, dims, preferred_element_type=F32)


def shifted(device, k, sign):
    core, y, x = device % 2, device // 2 % 4, device // 8
    dc, dy, dx = k % 2, k // 2 % 4, k // 8
    return ((x + sign * dx + 4) % 4 * 4 + (y + sign * dy + 4) % 4) * 2 + (core + dc) % 2


def plane_of(device):
    core, y, x = device % 2, device // 2 % 4, device // 8
    xs = [(x + d) % 4 * 8 for d in range(4)]
    ys = [(y + d) % 4 * 2 for d in range(4)]
    return [xs[k // 8] + ys[k // 2 % 4] + (core + k % 2) % 2 for k in range(PEERS)]


def iota(shape, axis):
    return lax.broadcasted_iota(jnp.int32, shape, axis)


def as_column(row):
    n = row.shape[1]
    return jnp.sum(jnp.where(iota((n, n), 0) == iota((n, n), 1), row, 0), axis=1, keepdims=True)


def as_lanes(column):
    n = column.shape[0]
    return jnp.sum(jnp.where(iota((n, LANES), 0) == iota((n, LANES), 1), column, 0), axis=0, keepdims=True)


def scattered(slot, value):
    return jnp.sum(jnp.where(slot == iota((slot.shape[0], LANES), 1), value, 0), axis=0, keepdims=True)


def kernel(
    orb_hbm, coeffs_hbm, amps_hbm, inter_hbm, energy_hbm, orbitals_hbm, nearby_hbm, rank_hbm, fock_hbm, weight_hbm,
    out, orbs, coeffs, amps, masked, inter, energy, orbitals, nearby, rank, fock, weight,
    first, exchange, coupled, outbox, inbox, asked, table, table_s, asked_s, local_sem, ring_out, ring_in, ask_out, ask_in, amp_out, amp_in,
):
    grp = lax.axis_index("grp")
    me = lax.axis_index("pair")
    right = lax.rem(grp + 1, GROUPS)
    left = lax.rem(grp + GROUPS - 1, GROUPS)

    def load(i, source, target):
        copy = pltpu.make_async_copy(source, target, local_sem.at[i])
        copy.start()
        return copy

    own_orbs = load(0, orb_hbm, orbs.at[0])
    own_nearby = load(1, nearby_hbm, nearby)
    own_orbitals = load(2, orbitals_hbm, orbitals)
    own_rank = load(3, rank_hbm, rank)

    barrier = pltpu.get_barrier_semaphore()
    for target in (right, left):
        pl.semaphore_signal(barrier, inc=1, device_id=(target, me), device_id_type=MESH)

    plane = plane_of(me)
    for k in range(1, PEERS):
        pl.semaphore_signal(barrier, inc=1, device_id=(grp, plane[k]), device_id_type=MESH)

    own_amps = load(4, amps_hbm, amps)
    own_coeffs = load(5, coeffs_hbm, coeffs)
    own_inter = load(6, inter_hbm, inter)
    own_energy = load(7, energy_hbm, energy)
    own_fock = load(8, fock_hbm, fock)
    own_weight = load(9, weight_hbm, weight)
    own_orbs.wait()
    own_nearby.wait()
    own_orbitals.wait()
    pl.semaphore_wait(barrier, PEERS + 1)

    def ring(d, s, c):
        chunk = c if d == 0 else CHUNKS - 1 - c
        rows = pl.ds(chunk * ROWS, ROWS)
        here = (GROUPS - (s - 1)) % GROUPS if d == 0 else s - 1
        there = GROUPS - s if d == 0 else s
        return pltpu.make_async_remote_copy(
            orbs.at[here, rows], orbs.at[there, rows], ring_out.at[d, s - 1, c], ring_in.at[d, s - 1, c],
            device_id=(right if d == 0 else left, me), device_id_type=MESH,
        )

    def ask(k):
        return pltpu.make_async_remote_copy(
            table.at[pl.ds(0, 1)], asked.at[pl.ds(k, 1)], ask_out.at[k], ask_in.at[k],
            device_id=(grp, plane[k] if isinstance(k, int) else shifted(me, k, 1)), device_id_type=MESH,
        )

    def answer(k):
        return pltpu.make_async_remote_copy(
            outbox.at[k], inbox.at[k], amp_out.at[k], amp_in.at[k],
            device_id=(grp, shifted(me, k, -1)), device_id_type=MESH,
        )

    @pl.loop(0, CHUNKS)
    def _(c):
        ring(0, 1, c).start()
        ring(1, 1, c).start()

    above = iota((PAIRS, PAIRS), 1) < iota((PAIRS, PAIRS), 0)

    def same(column, row):
        return column == row

    def count(hits):
        return jnp.sum(jnp.where(hits, 1, 0), axis=1, keepdims=True)

    def within(place):
        return jnp.minimum(place, SLOTS - 1)

    column_of = (nearby[...] >> 5) & (PEERS - 1)
    core, y, x = me % 2, me // 2 % 4, me // 8
    distance = (((column_of >> 3) - x) & 3) * 8 + ((((column_of >> 1) & 3) - y) & 3) * 2 + ((column_of - core) & 1)
    at = nearby[...] & (PAIRS - 1)
    rows = [distance[0:1], distance[1:2]]
    columns = [as_column(r) for r in rows]
    wanted = [as_column(at[0:1]), as_column(at[1:2])]
    place = [
        columns[0] * SLOTS + within(count(same(columns[0], rows[0]) & above)),
        columns[1] * SLOTS + within(count(same(columns[1], rows[0])) + count(same(columns[1], rows[1]) & above)),
    ]
    pair = iota((PAIRS, 1), 0)
    table[0:1] = (scattered(place[0], wanted[0]) + scattered(place[1], wanted[1])) & (PAIRS - 1)

    for k in range(1, PEERS):
        ask((k * STRIDE) % PEERS).start()

    table[1:2] = (scattered(place[0], 2 * pair) + scattered(place[1], 2 * pair + 1)) & (2 * PAIRS - 1)
    table[2:3] = as_lanes(place[0])
    table[3:4] = as_lanes(place[1])
    second = orbitals[1:2]
    home = ((second >> 6) - grp) & (GROUPS - 1)
    home_column = as_column(home)
    home_place = home_column * SLOTS + within(count(same(home_column, home) & above))
    table[4:5] = scattered(home_place, pair) & (PAIRS - 1)
    table[5:6] = scattered(home_place, as_column(second & 1))
    table[6:7] = as_lanes(home_place)
    table[7:8] = as_lanes(as_column(orbitals[0:1] & 1))
    to_scalar = load(10, table, table_s)
    own_amps.wait()
    own_rank.wait()

    def live(p):
        top = rank[p] * (R // 3)
        return (iota((R, R), 0) < top) & (iota((R, R), 1) < top)

    def mask_pair(p, _):
        mine = amps[p].astype(F32)
        masked[p] = jnp.where(live(p), mine, 0.0).astype(BF16)
        return 0

    lax.fori_loop(0, PAIRS, mask_pair, 0, unroll=4)
    to_scalar.wait()
    own_coeffs.wait()

    def first_pair(p, _):
        half = table_s[7, p]
        block = jnp.where(half == 1, orbs[0, AUX:], orbs[0, :AUX])
        first[p] = dot(coeffs[p], block, NT).astype(BF16)
        return 0


    def forward(s, c):
        for d in (0, 1):
            ring(d, s - 1, c).wait_recv()
            ring(d, s, c).start()

    @pl.loop(0, ASK_AT)
    def _(c):
        forward(2, c)

    @pl.loop(1, PEERS)
    def _(k):
        ask(k).wait_recv()

    load(11, asked, asked_s).wait()

    @pl.loop(1, PEERS)
    def _(i):
        k = (i * STRIDE) % PEERS
        blocks = [masked[asked_s[k, SLOTS * k + j]] for j in range(SLOTS)]
        for j in range(3):
            outbox[k, j] = jnp.concatenate([blocks[j], blocks[3][:, 32 * j : 32 * j + 32]], axis=1)
        answer(k).start()

    @pl.loop(ASK_AT, CHUNKS)
    def _(c):
        forward(2, c)

    lax.fori_loop(0, PAIRS, first_pair, 0, unroll=4)

    own_inter.wait()
    own_energy.wait()
    own_fock.wait()
    own_weight.wait()

    def exchange_block(kz):
        slots = [kz * SLOTS + j for j in range(SLOTS)]
        pairs = [table_s[4, slot] for slot in slots]
        halves = [table_s[5, slot] for slot in slots]
        moved = [
            dot(coeffs[p], jnp.where(half == 1, orbs[kz, AUX:], orbs[kz, :AUX]), NT).astype(BF16)
            for p, half in zip(pairs, halves)
        ]
        sums = [dot(first[p], m, NT) for p, m in zip(pairs, moved)]
        for slot, total in zip(slots, sums):
            exchange[slot] = total

    def couple(slots, blocks):
        turns = [inter[table_s[1, slot]] for slot in slots]
        halves = [dot(t, block, NN).astype(BF16) for t, block in zip(turns, blocks)]
        sums = [dot(half, t, NT) for half, t in zip(halves, turns)]
        for slot, total in zip(slots, sums):
            coupled[slot] = total

    def couple_own():
        couple(range(SLOTS), [masked[table_s[0, j]] for j in range(SLOTS)])

    def couple_peers(begin, n):
        slots, blocks = [], []
        for i in range(n):
            k = ((begin + i) * STRIDE) % PEERS
            answer(k).wait_recv()
            parts = [inbox[k, j] for j in range(3)]
            slots += [SLOTS * k + j for j in range(SLOTS)]
            blocks += [part[:, :R] for part in parts]
            blocks.append(jnp.concatenate([part[:, R:] for part in parts], axis=1))
        if n:
            couple(slots, blocks)

    def diagonal(p, _):
        across = energy[pl.ds(p, 1), :]
        down = jnp.sum(jnp.where(iota((R, R), 0) == iota((R, R), 1), across, 0.0), axis=1, keepdims=True)
        out[p] = (down + across - (fock[0, p] + fock[1, p])) * amps[p].astype(F32)
        return 0

    def exchange_side(s, side):
        exchange_block(jnp.where(side == 0, s, GROUPS - s))

    done = 1
    for low, high, n in PLAN:
        begin = done

        @pl.loop(low, high)
        def _(s):
            @pl.loop(0, 2)
            def _(h):
                forward(s, 2 * h)
                exchange_side(s - 2, h)
                forward(s, 2 * h + 1)
                couple_peers(begin + (2 * (s - low) + h) * n, n)

        done += (high - low) * 2 * n

        if low == 3:
            exchange_block(0)
            couple_own()
            lax.fori_loop(0, PAIRS, diagonal, 0, unroll=4)

    forward(HALF, 0)
    forward(HALF, 1)
    exchange_side(HALF - 2, 0)
    exchange_side(HALF - 2, 1)
    couple_peers(done, LAST)
    done += LAST

    for c in (2, 3):
        for d in (0, 1):
            ring(d, HALF - 1, c).wait_recv()

    @pl.loop(0, 2)
    def _(h):
        exchange_side(HALF - 1, h)

    @pl.loop(0, (PEERS - done) // 2)
    def _(i):
        couple_peers(done + 2 * i, 2)

    couple_peers(done + (PEERS - done) // 2 * 2, (PEERS - done) % 2)

    def settle(p, _):
        near = weight[0, p] * coupled[table_s[2, p]] + weight[1, p] * coupled[table_s[3, p]]
        out[p] = out[p] - near
        return 0

    lax.fori_loop(0, PAIRS, settle, 0, unroll=4)

    @pl.loop(0, 2)
    def _(c):
        ring(0, HALF, c).wait_recv()
        ring(1, HALF, c).wait_recv()

    exchange_block(HALF)

    def finish(p, _):
        out[p] = jnp.where(live(p), out[p] + exchange[table_s[6, p]], 0.0)
        return 0

    lax.fori_loop(0, PAIRS, finish, 0, unroll=4)

    @pl.loop(1, PEERS)
    def _(k):
        ask(k).wait_send()
        answer(k).wait_send()

    @pl.loop(1, HALF)
    def _(s):
        @pl.loop(0, CHUNKS)
        def _(c):
            ring(0, s, c).wait_send()
            ring(1, s, c).wait_send()

    @pl.loop(0, 2)
    def _(c):
        ring(0, HALF, c).wait_send()
        ring(1, HALF, c).wait_send()


def local(
    orbital_ints, pair_fock, pair_orbitals, rank_bucket, pno_coeffs, pno_energy, amplitudes, neighbors, intersections, coupling_fock
):
    operands = (
        orbital_ints.reshape(2 * AUX, AUX),
        jnp.swapaxes(pno_coeffs, 1, 2),
        amplitudes,
        intersections.reshape(2 * PAIRS, R, R),
        pno_energy,
        pair_orbitals.T,
        neighbors.T,
        rank_bucket,
        pair_fock.T,
        coupling_fock.T,
    )
    dma = pltpu.SemaphoreType.DMA
    return pl.pallas_call(
        kernel,
        out_shape=pltpu.VMEM((PAIRS, R, R), F32),
        in_specs=[pl.BlockSpec(memory_space=pltpu.HBM)] * 10,
        out_specs=pl.BlockSpec(memory_space=pltpu.VMEM),
        scratch_shapes=[
            pltpu.VMEM((GROUPS, 2 * AUX, AUX), BF16),
            pltpu.VMEM((PAIRS, R, AUX), BF16),
            pltpu.VMEM((PAIRS, R, R), BF16),
            pltpu.VMEM((PAIRS, R, R), BF16),
            pltpu.VMEM((2 * PAIRS, R, R), BF16),
            pltpu.VMEM((PAIRS, R), F32),
            pltpu.VMEM((2, PAIRS), jnp.int32),
            pltpu.VMEM((2, PAIRS), jnp.int32),
            pltpu.SMEM((PAIRS,), jnp.int32),
            pltpu.SMEM((2, PAIRS), F32),
            pltpu.SMEM((2, PAIRS), F32),
            pltpu.VMEM((PAIRS, R, AUX), BF16),
            pltpu.VMEM((GROUPS * SLOTS, R, R), F32),
            pltpu.VMEM((PEERS * SLOTS, R, R), F32),
            pltpu.VMEM((PEERS, 3, R, LANES), BF16),
            pltpu.VMEM((PEERS, 3, R, LANES), BF16),
            pltpu.VMEM((PEERS, LANES), jnp.int32),
            pltpu.VMEM((8, LANES), jnp.int32),
            pltpu.SMEM((8, LANES), jnp.int32),
            pltpu.SMEM((PEERS, LANES), jnp.int32),
            dma((12,)),
            dma((2, HALF, CHUNKS)),
            dma((2, HALF, CHUNKS)),
            dma((PEERS,)),
            dma((PEERS,)),
            dma((PEERS,)),
            dma((PEERS,)),
        ],
        compiler_params=pltpu.CompilerParams(
            collective_id=0, has_side_effects=True, vmem_limit_bytes=48 * 2**20
        ),
    )(*[pltpu.with_memory_space_constraint(operand, pltpu.HBM) for operand in operands])


def solution(mesh):
    rows = P(("grp", "pair"))
    return jax.shard_map(
        local,
        mesh=mesh,
        in_specs=(rows,) * 10,
        out_specs=rows,
        check_vma=False,
    )
```
